128 devices in a mesh: tile: 32 (over y_hi, x, z), var: 4 (over y_lo, core).
Axes of the slice: x: 4, y: 4 (y_hi: 2, y_lo: 2; y = y_hi * 2 + y_lo), z: 4, core: 2. Of those that a mesh axis runs over, the one named last changes fastest.
Arguments:
- tokens: bfloat16 [32768, 3072], P('tile', 'var'), may hold values from -6 to 6
- norm_gain: float32 [3072], replicated, may hold values from 0.1 to 1.9
- query_weight: bfloat16 [3072, 3072], P('tile', 'var'), may hold values from -48 to 48
- key_weight: bfloat16 [3072, 3072], P('tile', 'var'), may hold values from -1 to 1
- value_weight: bfloat16 [3072, 3072], P('tile', 'var'), may hold values from -0.109375 to 0.109375
- out_weight: bfloat16 [3072, 3072], P('tile', 'var'), may hold values from -0.109375 to 0.109375
- head_gain: float32 [3072], replicated, may hold values from 0.1 to 1.9
- head_weight: bfloat16 [3072, 1024], P('tile', 'var'), may hold values from -0.109375 to 0.109375
Outputs:
- fields: float32 [32768, 1024], P('tile', 'var')
The draws below stay inside these ranges and needn't reach their ends.
All inputs are finite; a program needn't handle non-finite values.
Results may differ from the reference program's by a relative error of at most 0.0095.
Values may be sent and summed in bfloat16 or wider, within the bound.
No kernel may reach another device: no remote copies, remote signals or barrier semaphores. Data moves between devices by JAX's collectives and lax.ppermute only.
A program may use at most 128 MiB of HBM per device.

```python
import math
import jax
import jax.numpy as jnp
from jax import lax

D = 3072
HEADS = 24
VARS = 64
PIX = 16
ROWS = 8
LAT = 128
HD = 128
NLON = 256
TOKENS = 32768
N_TILE = 32


def shared_base(key):
    return jnp.clip(jax.random.normal(key, (D, D), jnp.float32), -4.0, 4.0)


def draw_key_weight(key, part):
    base = shared_base(key)
    return (base * (1.0 / math.sqrt(D))).astype(jnp.bfloat16)


def draw_query_weight(key, part):
    key = jax.random.fold_in(key, 5)
    own_key = jax.random.fold_in(key, 0)
    weights = jnp.clip(jax.random.normal(own_key, (D, D), jnp.float32), -4.0, 4.0) * (1.0 / math.sqrt(D // 8))
    return weights.astype(jnp.bfloat16)


def draw_tokens(key, part):
    key = jax.random.fold_in(key, 7)
    first_key = jax.random.fold_in(key, 0)
    return jnp.clip(jax.random.normal(first_key, (TOKENS, D), jnp.float32), -6.0, 6.0).astype(jnp.bfloat16)


def block_levels(stream_key, extent, cuts, smallest, top_value):
    def one(position, parts):
        draws = jax.random.uniform(jax.random.fold_in(jax.random.fold_in(stream_key, 6), position), (parts,), jnp.float32, smallest / len(cuts), top_value / len(cuts))
        return jnp.repeat(jnp.exp(draws), extent[position] // parts).reshape((-1,) + (1,) * (len(extent) - position - 1))

    level = one(*cuts[0])
    for cut in cuts[1:]:
        level = level * one(*cut)
    return level


def bell_draw(key, extent, scale, limit, shards=(), kind=jnp.bfloat16):
    drawn = jax.random.normal(key, extent, jnp.float32) * scale
    if len(shards) > 0:
        drawn = block_levels(key, extent, shards, -0.22, 0.18) * drawn
    return jnp.clip(drawn, min=-limit, max=limit).astype(kind)


def setup_inputs(seed: int = 0) -> dict:
    arg_keys = jax.random.split(jax.random.key(seed), 9)
    return {
        "tokens": draw_tokens(jax.random.fold_in(arg_keys[8], 71), 0),
        "norm_gain": jnp.clip(1.0 + 0.18 * jax.random.normal(arg_keys[1], (D,), jnp.float32), 0.1, 1.9),
        "query_weight": draw_query_weight(jax.random.fold_in(arg_keys[8], 71), 0),
        "key_weight": draw_key_weight(jax.random.fold_in(arg_keys[8], 71), 0),
        "value_weight": bell_draw(arg_keys[4], (D, D), D ** -0.5, 0.109375, ((0, 32), (1, 4))),
        "out_weight": bell_draw(arg_keys[5], (D, D), D ** -0.5, 0.109375, ((0, 32), (1, 4))),
        "head_gain": jnp.clip(1.0 + 0.18 * jax.random.normal(arg_keys[6], (D,), jnp.float32), 0.1, 1.9),
        "head_weight": bell_draw(arg_keys[7], (D, VARS * PIX), D ** -0.5, 0.109375, ((0, 32), (1, 4))),
    }


def layer_norm(values, gain):
    values = values.astype(jnp.float32)
    center = values - lax.optimization_barrier(jnp.mean(values, axis=-1, keepdims=True))
    spread = lax.optimization_barrier(jnp.mean(center * center, axis=-1, keepdims=True))
    return center * lax.rsqrt(spread + 1e-05) * gain

def reference(tokens, norm_gain, query_weight, key_weight, value_weight, out_weight, head_gain, head_weight):
    normed = layer_norm(tokens, norm_gain).astype(jnp.bfloat16)
    queries = jnp.dot(normed, query_weight, preferred_element_type=jnp.float32).astype(jnp.bfloat16)
    keys = jnp.dot(normed, key_weight, preferred_element_type=jnp.float32).astype(jnp.bfloat16)
    values = jnp.dot(normed, value_weight, preferred_element_type=jnp.float32).astype(jnp.bfloat16)
    key_grid = keys.reshape(NLON, LAT, D)
    value_grid = values.reshape(NLON, LAT, D)
    key_grid = jnp.concatenate([key_grid[-1:], key_grid, key_grid[:1]], axis=0)
    value_grid = jnp.concatenate([value_grid[-1:], value_grid, value_grid[:1]], axis=0)
    query_tiles = queries.reshape(N_TILE, ROWS * LAT, HEADS, HD)

    def one_tile(index):
        first = (index * ROWS).astype(jnp.int32)
        near_keys = lax.dynamic_slice_in_dim(key_grid, first, ROWS + 2, 0).reshape((ROWS + 2) * LAT, HEADS, HD)
        near_values = lax.dynamic_slice_in_dim(value_grid, first, ROWS + 2, 0).reshape((ROWS + 2) * LAT, HEADS, HD)
        query_block = query_tiles[index].astype(jnp.float32)
        scores = jnp.einsum('qhd,khd->hqk', query_block, near_keys.astype(jnp.float32)) / jnp.sqrt(jnp.float32(HD))
        probs = jax.nn.softmax(scores, axis=-1).astype(jnp.bfloat16)
        mixed = jnp.einsum('hqk,khd->qhd', probs.astype(jnp.float32), near_values.astype(jnp.float32))
        return mixed.reshape(ROWS * LAT, D).astype(jnp.bfloat16)
    attended = lax.map(one_tile, jnp.arange(N_TILE, dtype=jnp.int32)).reshape(TOKENS, D)
    resid = (tokens.astype(jnp.float32) + jnp.dot(attended, out_weight, preferred_element_type=jnp.float32)).astype(jnp.bfloat16)
    head_input = layer_norm(resid, head_gain).astype(jnp.bfloat16)
    return jnp.dot(head_input, head_weight, preferred_element_type=jnp.float32)
```

```python
import math

import jax
import jax.numpy as jnp
from jax import lax
from jax.experimental import pallas as pl
from jax.experimental.pallas import tpu as pltpu
from jax.sharding import PartitionSpec as P

D = 3072
HD = 128
LAT = 128
TILE = 1024
BLOCK = 768
OWN = 384
EPS = 1e-05
AXES = ("tile", "var")
SCALE = math.log2(math.e) / math.sqrt(HD)
F32 = jnp.float32
BF16 = jnp.bfloat16


def device(yh, x, z, yl, c):
    return ((yh % 2) * 16 + (x % 4) * 4 + (z % 4)) * 4 + (yl % 2) * 2 + (c % 2)


def pairs(move):
    return [
        (device(yh, x, z, yl, c), device(*move(yh, x, z, yl, c)))
        for yh in range(2)
        for x in range(4)
        for z in range(4)
        for yl in range(2)
        for c in range(2)
    ]


def send(value, move):
    return lax.ppermute(value, AXES, pairs(move))


def other_core(yh, x, z, yl, c):
    return yh, x, z, yl, c + 1


def near(yh, x, z, yl, c):
    return yh, x, z, yl + 1, c


def near_other_core(yh, x, z, yl, c):
    return yh, x, z, yl + 1, c + 1


def far(yh, x, z, yl, c):
    return yh + 1, x, z, yl, c


def diagonal(yh, x, z, yl, c):
    return yh + 1, x, z, yl + 1, c


def along(first, step):
    def move(yh, x, z, yl, c):
        if (c == 0) == first:
            return yh, x, z + step, yl, c
        return yh, x + step, z, yl, c

    return move


def next_place(step):
    def move(yh, x, z, yl, c):
        place = (x * 4 + z + step) % 16
        return yh, place // 4, place % 4, yl, c

    return move


def call(kernel, out_shape, *args, scalars=None, specs=None, scratch=(), flops=0, grid=(), out_specs=None, limit=48):
    whole = pl.BlockSpec(memory_space=pltpu.VMEM)
    specs = specs or [whole] * len(args)
    out_specs = out_specs or jax.tree.map(lambda _: whole, out_shape)
    moved = sum(math.prod(a.shape) * a.dtype.itemsize for a in (*args, *jax.tree.leaves(out_shape)))
    return pl.pallas_call(
        kernel,
        out_shape=out_shape,
        grid_spec=pltpu.PrefetchScalarGridSpec(
            num_scalar_prefetch=1,
            grid=grid,
            in_specs=specs,
            out_specs=out_specs,
            scratch_shapes=scratch,
        ),
        compiler_params=pltpu.CompilerParams(vmem_limit_bytes=limit * 2**20),
        cost_estimate=pl.CostEstimate(flops=flops, bytes_accessed=moved, transcendentals=0),
    )(scalars, *args)


def project(scalars, blocks, pieces):
    counts = [len(b) for b in blocks]
    places = [(0, range(4)), (1, range(4)), (2, range(4)), (3, range(2)), (3, range(2, 4))]

    def kernel(s_ref, *refs):
        x_refs = []
        at = 0
        for n in counts:
            x_refs.append(refs[at : at + n])
            at += n
        w_refs = refs[at : at + 5]
        out_ref, w, sem = refs[at + 5 :]
        copies = []
        for ref, (i, ks) in zip(w_refs, places):
            for n, k in enumerate(ks):
                piece = i * 4 + k
                copies.append(pltpu.make_async_copy(ref.at[n], w.at[s_ref[4 + piece]], sem.at[piece]))
        for copy in copies:
            copy.start()
        for copy in copies:
            copy.wait()
        for m in range(4):
            for n in range(3):
                total = None
                for r in range(4):
                    v = s_ref[r]
                    rows = TILE // counts[r]
                    x = x_refs[r][m * 256 // rows][pl.ds(m * 256 % rows, 256), :]
                    lanes = pl.ds(pl.multiple_of((v // 2) * 1152 + n * OWN, 128), OWN)
                    weight = w[pl.ds((v % 2) * 8, 8), :, lanes].reshape(BLOCK, OWN)
                    part = jnp.dot(x, weight, preferred_element_type=F32)
                    total = part if total is None else total + part
                out_ref[pl.ds(m * 256, 256), pl.ds(n * OWN, OWN)] = total.astype(BF16)

    flat = [piece for b in blocks for piece in b]
    specs = [pl.BlockSpec(memory_space=pltpu.VMEM)] * len(flat) + [pl.BlockSpec(memory_space=pl.ANY)] * 5
    return call(
        kernel,
        jax.ShapeDtypeStruct((TILE, 3 * OWN), BF16),
        *flat,
        *pieces,
        scalars=scalars,
        specs=specs,
        scratch=[pltpu.VMEM((16, 96, 2304), BF16), pltpu.SemaphoreType.DMA((16,))],
        flops=2 * TILE * D * 3 * OWN,
    )


def attend(scalars, qkv, left, right):
    def kernel(s_ref, q_ref, k_ref, v_ref, lk, lv, lk2, lv2, rk, rv, rk2, rv2, out_ref, keys, values):
        swap_left = s_ref[0] == 1
        swap_right = s_ref[1] == 1
        keys[0:LAT, :] = jnp.where(swap_left, lk2[...], lk[...])
        keys[LAT : LAT + TILE, :] = k_ref[...]
        keys[LAT + TILE :, :] = jnp.where(swap_right, rk2[...], rk[...])
        values[0:LAT, 0:HD] = jnp.where(swap_left, lv2[...], lv[...])
        values[LAT : LAT + TILE, 0:HD] = v_ref[...]
        values[LAT + TILE :, 0:HD] = jnp.where(swap_right, rv2[...], rv[...])
        values[:, HD:] = jnp.ones((TILE + 2 * LAT, HD), BF16)
        for m in range(4):
            rows = pl.ds(m * 256, 256)
            scores = lax.dot_general(
                q_ref[rows, :], keys[...], (((1,), (1,)), ((), ())), preferred_element_type=F32
            )
            top = jnp.max(scores, axis=-1, keepdims=True)
            probs = jnp.exp2((scores - top) * SCALE).astype(BF16)
            mixed = jnp.dot(probs, values[...], preferred_element_type=F32)
            out_ref[rows, :] = (mixed[:, :HD] / mixed[:, HD:]).astype(BF16)

    def column(rows, first):
        return pl.BlockSpec((rows, HD), lambda h, s: (0, first + h))

    rims = [column(LAT, 0), column(LAT, 3)] * 4
    return call(
        kernel,
        jax.ShapeDtypeStruct((TILE, OWN), BF16),
        qkv,
        qkv,
        qkv,
        left[0],
        left[0],
        left[1],
        left[1],
        right[0],
        right[0],
        right[1],
        right[1],
        scalars=scalars,
        specs=[column(TILE, 0), column(TILE, 3), column(TILE, 6)] + rims,
        out_specs=column(TILE, 0),
        scratch=[pltpu.VMEM((TILE + 2 * LAT, HD), BF16), pltpu.VMEM((TILE + 2 * LAT, 2 * HD), BF16)],
        flops=4 * TILE * 1280 * OWN,
        grid=(3,),
    )


def out_project(scalars, tokens, blocks, weights):
    def kernel(s_ref, *refs):
        a_refs = refs[:8]
        t_ref, w_ref, out_ref = refs[8:]
        for m in range(4):
            rows = pl.ds(m * 256, 256)
            total = t_ref[rows, :].astype(F32)
            for r in range(8):
                j = s_ref[r]
                lanes = pl.ds(pl.multiple_of((j // 4) * BLOCK, 128), BLOCK)
                weight = w_ref[pl.ds(pl.multiple_of((j % 4) * OWN, 128), OWN), lanes]
                total = total + jnp.dot(a_refs[r][rows, :], weight, preferred_element_type=F32)
            out_ref[rows, :] = total.astype(BF16)

    return call(
        kernel,
        jax.ShapeDtypeStruct((TILE, BLOCK), BF16),
        *blocks,
        tokens,
        weights,
        scalars=scalars,
        specs=[pl.BlockSpec(memory_space=pltpu.VMEM)] * 9
        + [pl.BlockSpec((1536, 1536), lambda i, s: (0, 0))],
        out_specs=pl.BlockSpec((TILE, BLOCK), lambda i, s: (0, 0)),
        flops=2 * TILE * D * BLOCK,
        grid=(1,),
    )


def head_partial(scalars, first, second, gain, weights):
    def kernel(s_ref, a_ref, b_ref, g_ref, w_ref, keep_ref, send_ref, own_ref, sent_ref):
        own = pl.ds(pl.multiple_of(s_ref[0] * 256, 256), 256)
        other = pl.ds(pl.multiple_of((1 - s_ref[0]) * 256, 256), 256)
        gain = g_ref[...]
        gain_high = gain.astype(BF16)
        gain_low = (gain - gain_high.astype(F32)).astype(BF16)
        shift = jnp.dot(jnp.concatenate([gain_high, gain_low], axis=0), w_ref[...], preferred_element_type=F32)
        shift = shift[0:8] + shift[8:16]
        keep_ref[pl.ds(TILE, 8), :] = jnp.where(s_ref[0] == 0, shift[:, :256], shift[:, 256:])
        columns = []
        for m in range(4):
            rows = pl.ds(m * 256, 256)
            a = a_ref[rows, :].astype(F32)
            b = b_ref[rows, :].astype(F32)
            mean = (jnp.sum(a, axis=-1, keepdims=True) + jnp.sum(b, axis=-1, keepdims=True)) * (1.0 / 1536)
            a = a - mean
            b = b - mean
            spread = jnp.sum(a * a, axis=-1, keepdims=True) + jnp.sum(b * b, axis=-1, keepdims=True)
            a = (a * gain[0:1, :BLOCK]).astype(BF16)
            b = (b * gain[0:1, BLOCK:]).astype(BF16)
            for lanes, target in ((own, keep_ref), (other, send_ref)):
                part = jnp.dot(a, w_ref[0:BLOCK, lanes], preferred_element_type=F32)
                part += jnp.dot(b, w_ref[BLOCK:, lanes], preferred_element_type=F32)
                target[rows, :] = part.astype(target.dtype)
            place = lax.broadcasted_iota(jnp.int32, (256, 128), 1)
            columns.append(jnp.where(place == 0, mean, jnp.where(place == 1, spread, 0.0)))
        stats = jnp.transpose(jnp.concatenate(columns, axis=0))[0:8]
        own_ref[...] = stats
        sent = jnp.where(s_ref[0] == 0, shift[:, 256:], shift[:, :256])
        line = lax.broadcasted_iota(jnp.int32, (8, 256), 0)
        sent_ref[:, 256:] = stats[:, 256:]
        sent_ref[:, :256] = stats[:, :256] + jnp.where(line == 2, sent, 0.0)

    return call(
        kernel,
        (
            jax.ShapeDtypeStruct((TILE + 8, 256), F32),
            jax.ShapeDtypeStruct((TILE, 256), BF16),
            jax.ShapeDtypeStruct((8, TILE), F32),
            jax.ShapeDtypeStruct((8, TILE), F32),
        ),
        first,
        second,
        gain,
        weights,
        scalars=scalars,
        specs=[pl.BlockSpec(memory_space=pltpu.VMEM)] * 3 + [pl.BlockSpec((1536, 512), lambda i, s: (0, 3))],
        flops=2 * TILE * 1536 * 512,
        grid=(1,),
    )


def combine(scalars, kept, received, own, theirs):
    def kernel(s_ref, k_ref, r_ref, o_ref, t_ref, out_ref):
        pad = jnp.zeros((112, TILE), F32)
        both = jnp.transpose(jnp.concatenate([o_ref[...], t_ref[...], pad], axis=0))
        mean_a, spread_a = both[:, 0:1], both[:, 1:2]
        mean_b, spread_b = both[:, 8:9], both[:, 9:10]
        half = (mean_a - mean_b) * 0.5
        spread = (spread_a + spread_b + half * half * D) * (1.0 / D)
        scale = lax.rsqrt(spread + EPS)
        shift = k_ref[pl.ds(TILE, 8), :][0:1] - t_ref[...][2:3, :256]
        out_ref[...] = (k_ref[pl.ds(0, TILE), :] + r_ref[...].astype(F32) + half * shift) * scale

    return call(kernel, jax.ShapeDtypeStruct((TILE, 256), F32), kept, received, own, theirs, scalars=scalars)


def gather_pieces(shard):
    from_left = send(shard, along(True, 1))
    from_right = send(shard, along(True, -1))
    from_far = send(shard, along(True, 2))
    line = jnp.stack([shard, from_left, from_right, from_far])
    left = send(line, along(False, 1))
    right = send(line, along(False, -1))
    far_left = send(left[:2], along(False, 1))
    far_right = send(right[2:], along(False, -1))
    return line, left, right, far_left, far_right


def shards(
    tokens, norm_gain, query_weight, key_weight, value_weight, out_weight, head_gain, head_weight
):
    tile = lax.axis_index("tile")
    var = lax.axis_index("var")
    yh, place = tile // 16, tile % 16
    x, z = place // 4, place % 4
    yl, c = var // 2, var % 2

    qkv_weight = jnp.concatenate(
        [w.reshape(96, 2, OWN) for w in (query_weight, key_weight, value_weight)], axis=-1
    )
    low, high = qkv_weight[:, 0], qkv_weight[:, 1]
    first = yh == 0
    mine = jnp.where(first, low, high)
    rest = jnp.where(first, high, low)
    got = send(jnp.concatenate([rest, out_weight, head_weight], axis=1), far)
    qkv_other, out_other, head_other = got[:, :1152], got[:, 1152:1920], got[:, 1920:]
    shard = jnp.where(
        first, jnp.concatenate([mine, qkv_other], axis=1), jnp.concatenate([qkv_other, mine], axis=1)
    )
    same = yh == yl
    head_mine = jnp.where(same, head_weight, head_other)
    head_got = send(jnp.where(same, head_other, head_weight), near)
    late = jnp.concatenate(
        [
            jnp.where(first, out_weight, out_other),
            jnp.where(first, out_other, out_weight),
            jnp.where(yl == 0, head_mine, head_got),
            jnp.where(yl == 0, head_got, head_mine),
        ],
        axis=1,
    )
    groups = [list(range(0, 16)), list(range(16, 32))]
    late_weights = lax.all_gather(late, "tile", axis_index_groups=groups, axis=0, tiled=True)

    raw = tokens.astype(F32)
    mean = jnp.mean(raw, axis=-1)
    spread = jnp.sum((raw - mean[:, None]) ** 2, axis=-1)
    stats = jnp.stack([mean, spread])
    all_stats = [stats, send(stats, other_core), send(stats, near), send(stats, near_other_core)]
    total_mean = (all_stats[0][0] + all_stats[1][0] + all_stats[2][0] + all_stats[3][0]) * 0.25
    total = sum(s[1] + BLOCK * (s[0] - total_mean) ** 2 for s in all_stats) * (1.0 / D)
    gain = lax.dynamic_slice_in_dim(norm_gain, var * BLOCK, BLOCK)
    normed = ((raw - total_mean[:, None]) * lax.rsqrt(total + EPS)[:, None] * gain).astype(BF16)

    near_block = send(normed, near)
    diagonal_block = send(normed, diagonal)
    far_top = send(diagonal_block[:512], near)
    far_bottom = send(near_block[512:], diagonal)
    pieces = gather_pieces(shard)

    offsets = jnp.array([0, -1, 1, 2], jnp.int32)
    second, primary = jnp.meshgrid(offsets, offsets, indexing="ij")
    place_z = jnp.where(c == 0, z + primary, z + second) % 4
    place_x = jnp.where(c == 0, x + second, x + primary) % 4
    piece_place = (place_x * 4 + place_z).reshape(16)

    def tables(half):
        return jnp.concatenate(
            [jnp.stack([2 * half + c, 2 * half + 1 - c, 2 * (1 - half) + c, 2 * (1 - half) + 1 - c]), piece_place]
        ).astype(jnp.int32)

    flip = lambda value: send(value, other_core)
    own_qkv = project(
        tables(yl), [[normed], [flip(normed)], [near_block], [flip(near_block)]], pieces
    )
    rest_qkv = project(
        tables(1 - yl),
        [
            [diagonal_block],
            [flip(diagonal_block)],
            [far_top, far_bottom],
            [flip(far_top), flip(far_bottom)],
        ],
        pieces,
    )

    own_left = send(own_qkv[-LAT:, OWN:], next_place(1))
    own_right = send(own_qkv[:LAT, OWN:], next_place(-1))
    rest_left = send(rest_qkv[-LAT:, OWN:], next_place(1))
    rest_right = send(rest_qkv[:LAT, OWN:], next_place(-1))
    swaps = jnp.stack([place == 0, place == 15]).astype(jnp.int32)
    rest_attended = attend(swaps, rest_qkv, (rest_left, own_left), (rest_right, own_right))
    from_far = send(rest_attended, far)
    from_diagonal = send(rest_attended, diagonal)
    own_attended = attend(swaps, own_qkv, (own_left, rest_left), (own_right, rest_right))
    from_near = send(own_attended, near)

    blocks = []
    for block in (own_attended, from_far, from_diagonal, from_near):
        blocks += [block, flip(block)]
    ids = [
        (2 * half + core) * 2 + high_half
        for half, high_half in ((yl, yh), (yl, 1 - yh), (1 - yl, 1 - yh), (1 - yl, yh))
        for core in (c, 1 - c)
    ]
    resid = out_project(jnp.stack(ids).astype(jnp.int32), tokens, blocks, late_weights)

    resid_other = flip(resid)
    low_core = c == 0
    chip_gain = lax.dynamic_slice_in_dim(head_gain, yl * 1536, 1536)
    kept, leaving, own_stats, leaving_stats = head_partial(
        jnp.stack([yl]).astype(jnp.int32),
        jnp.where(low_core, resid, resid_other),
        jnp.where(low_core, resid_other, resid),
        jnp.broadcast_to(chip_gain[None], (8, 1536)),
        late_weights,
    )
    received = send(leaving, near)
    their_stats = send(leaving_stats, near)
    return combine(jnp.zeros((1,), jnp.int32), kept, received, own_stats, their_stats)


def solution(mesh):
    return jax.shard_map(
        shards,
        mesh=mesh,
        in_specs=(
            P("tile", "var"),
            P(),
            P("tile", "var"),
            P("tile", "var"),
            P("tile", "var"),
            P("tile", "var"),
            P(),
            P("tile", "var"),
        ),
        out_specs=P("tile", "var"),
        check_vma=False,
    )
```

```python
import math

import jax
import jax.numpy as jnp
from jax import lax
from jax.experimental import pallas as pl
from jax.experimental.pallas import tpu as pltpu
from jax.sharding import PartitionSpec as P

D = 3072
HD = 128
LAT = 128
TILE = 1024
BLOCK = 768
OWN = 384
EPS = 1e-05
AXES = ("tile", "var")
SCALE = math.log2(math.e) / math.sqrt(HD)
F32 = jnp.float32
BF16 = jnp.bfloat16


def device(yh, x, z, yl, c):
    return ((yh % 2) * 16 + (x % 4) * 4 + (z % 4)) * 4 + (yl % 2) * 2 + (c % 2)


def pairs(move):
    return [
        (device(yh, x, z, yl, c), device(*move(yh, x, z, yl, c)))
        for yh in range(2)
        for x in range(4)
        for z in range(4)
        for yl in range(2)
        for c in range(2)
    ]


def send(value, move):
    return lax.ppermute(value, AXES, pairs(move))


def other_core(yh, x, z, yl, c):
    return yh, x, z, yl, c + 1


def near(yh, x, z, yl, c):
    return yh, x, z, yl + 1, c


def near_other_core(yh, x, z, yl, c):
    return yh, x, z, yl + 1, c + 1


def far(yh, x, z, yl, c):
    return yh + 1, x, z, yl, c


def diagonal(yh, x, z, yl, c):
    return yh + 1, x, z, yl + 1, c


def along(first, step):
    def move(yh, x, z, yl, c):
        if (c == 0) == first:
            return yh, x, z + step, yl, c
        return yh, x + step, z, yl, c

    return move


def next_place(step):
    def move(yh, x, z, yl, c):
        place = (x * 4 + z + step) % 16
        return yh, place // 4, place % 4, yl, c

    return move


def call(kernel, out_shape, *args, scalars, specs=None, scratch=(), flops=0, grid=(), out_specs=None, limit=16):
    whole = pl.BlockSpec(memory_space=pltpu.VMEM)
    out_specs = out_specs or jax.tree.map(lambda _: whole, out_shape)
    return pl.pallas_call(
        kernel,
        out_shape=out_shape,
        grid_spec=pltpu.PrefetchScalarGridSpec(
            num_scalar_prefetch=1,
            grid=grid,
            in_specs=specs or [whole] * len(args),
            out_specs=out_specs,
            scratch_shapes=scratch,
        ),
        compiler_params=pltpu.CompilerParams(vmem_limit_bytes=limit * 2**20),
        cost_estimate=pl.CostEstimate(flops=flops, bytes_accessed=flops // 512, transcendentals=0),
    )(scalars, *args)


ANY = pl.BlockSpec(memory_space=pl.ANY)
INNER = pl.BlockSpec(memory_space=pltpu.VMEM)
def joined(parts, *others):
    total = sum(n for _, _, n in parts)
    shape = parts[0][0].shape

    def kernel(s_ref, *refs):
        out_ref, sem = refs[-2:]
        copies = []
        at = 0
        for i, (_, start, n) in enumerate(parts):
            copies.append(
                pltpu.make_async_copy(refs[i].at[pl.ds(start, n)], out_ref.at[pl.ds(at, n)], sem.at[i])
            )
            copies[-1].start()
            at += n
        for copy in copies:
            copy.wait()

    args = [part[0] for part in parts] + list(others)
    return call(
        kernel,
        jax.ShapeDtypeStruct((total,) + shape[1:], parts[0][0].dtype),
        *args,
        scalars=jnp.zeros((1,), jnp.int32),
        specs=[ANY] * len(args),
        scratch=[pltpu.SemaphoreType.DMA((len(parts),))],
    )


def leaving_weights(scalars, *weights):
    def kernel(s_ref, q_ref, k_ref, v_ref, o_ref, h_ref, mine_ref, send_ref):
        own = pl.ds(pl.multiple_of(s_ref[0] * OWN, 128), OWN)
        other = pl.ds(pl.multiple_of((1 - s_ref[0]) * OWN, 128), OWN)
        for i, ref in enumerate((q_ref, k_ref, v_ref)):
            mine_ref[:, pl.ds(i * OWN, OWN)] = ref[:, own]
            send_ref[:, pl.ds(i * OWN, OWN)] = ref[:, other]
        send_ref[:, 1152:1920] = o_ref[...]
        send_ref[:, 1920:] = h_ref[...]

    return call(
        kernel,
        (jax.ShapeDtypeStruct((96, 1152), BF16), jax.ShapeDtypeStruct((96, 2176), BF16)),
        *weights,
        scalars=scalars,
    )


def paired_weights(scalars, mine, got, head_weight, *others):
    def kernel(s_ref, m_ref, g_ref, h_ref, *refs):
        shard_ref, keep_ref, send_ref = refs[len(others) :]
        yh, same = s_ref[0], s_ref[0] == s_ref[1]
        shard_ref[:, pl.ds(pl.multiple_of(yh * 1152, 128), 1152)] = m_ref[...]
        shard_ref[:, pl.ds(pl.multiple_of((1 - yh) * 1152, 128), 1152)] = g_ref[:, :1152]
        keep_ref[...] = jnp.where(same, h_ref[...], g_ref[:, 1920:])
        send_ref[:, :256] = jnp.where(same, g_ref[:, 1920:], h_ref[...])
        send_ref[:, 256:] = jnp.zeros((96, 512), BF16)

    return call(
        kernel,
        (
            jax.ShapeDtypeStruct((96, 2304), BF16),
            jax.ShapeDtypeStruct((96, 256), BF16),
            jax.ShapeDtypeStruct((96, BLOCK), BF16),
        ),
        mine,
        got,
        head_weight,
        *others,
        scalars=scalars,
        specs=[INNER] * 3 + [ANY] * len(others),
    )


def late_rows(scalars, out_weight, got, keep, near_rim, *others):
    def kernel(s_ref, o_ref, g_ref, k_ref, n_ref, *refs):
        yh, yl = s_ref[0], s_ref[1]
        out_ref = refs[-1]
        out_ref[:, pl.ds(pl.multiple_of(yh * BLOCK, 128), BLOCK)] = o_ref[...]
        out_ref[:, pl.ds(pl.multiple_of((1 - yh) * BLOCK, 128), BLOCK)] = g_ref[:, 1152:1920]
        out_ref[:, pl.ds(pl.multiple_of(1536 + yl * 256, 128), 256)] = k_ref[...]
        out_ref[:, pl.ds(pl.multiple_of(1792 - yl * 256, 128), 256)] = n_ref[256:, :256]

    return call(
        kernel,
        jax.ShapeDtypeStruct((96, 2048), BF16),
        out_weight,
        got,
        keep,
        near_rim,
        *others,
        scalars=scalars,
        specs=[INNER] * 4 + [ANY] * len(others),
    )


PIECES = [range(0, 4), range(4, 8), range(8, 12), range(12, 14), range(14, 16)]


def load_weights(s_ref, refs, target, part, first, width, sem, base):
    lanes = pl.ds(pl.multiple_of(part * 1152 + first, 128), width)
    copies = []
    for ref, numbers in zip(refs, PIECES):
        for n, piece in enumerate(numbers):
            place = pl.ds(pl.multiple_of(s_ref[4 + piece] * 96, 96), 96)
            copies.append(
                pltpu.make_async_copy(ref.at[pl.ds(n * 96, 96), lanes], target.at[place, lanes], sem.at[base + piece])
            )
            copies[-1].start()
    return copies


def weight_of(w, v, first, width):
    lanes = pl.ds(pl.multiple_of((v // 2) * 1152 + first, 128), width)
    return w[pl.ds(pl.multiple_of((v % 2) * BLOCK, 128), BLOCK), lanes]


def project(scalars, sources, plan, pieces):
    steps = [(r,) + entry for r in range(4) for entry in plan[r]]

    def kernel(s_ref, *refs):
        at = len(sources)
        x_refs = refs[:at]
        w_refs = refs[at : at + 5]
        out_ref, w, x, sums, w_sem, x_sem = refs[at + 5 :]
        low = s_ref[0] // 2
        w_copies = []
        x_copies = []
        for part in range(2):
            w_copies.append(load_weights(s_ref, w_refs, w, low if part == 0 else 1 - low, 0, 1152, w_sem, part * 16))
            for m in range(4):
                for i, (r, source, start, target, n) in enumerate(steps):
                    if target // 256 == m and r // 2 == part:
                        copy = pltpu.make_async_copy(
                            x_refs[source].at[pl.ds(start, n)], x.at[r, pl.ds(target, n)], x_sem.at[i]
                        )
                        copy.start()
                        x_copies.append((part, m, copy))
        for part in range(2):
            for copy in w_copies[part]:
                copy.wait()
            for m in range(4):
                for at_part, step, copy in x_copies:
                    if at_part == part and step == m:
                        copy.wait()
                rows = pl.ds(m * 256, 256)
                total = None
                for r in (2 * part, 2 * part + 1):
                    product = jnp.dot(x[r, rows, :], weight_of(w, s_ref[r], 0, 1152), preferred_element_type=F32)
                    total = product if total is None else total + product
                if part == 0:
                    sums[rows, :] = total
                else:
                    out_ref[rows, :] = (total + sums[rows, :]).astype(BF16)

    args = [*sources, *pieces]
    return call(
        kernel,
        jax.ShapeDtypeStruct((TILE, 3 * OWN), BF16),
        *args,
        scalars=scalars,
        specs=[ANY] * len(args),
        scratch=[
            pltpu.VMEM((1536, 2304), BF16),
            pltpu.VMEM((4, TILE, BLOCK), BF16),
            pltpu.VMEM((TILE, 3 * OWN), F32),
            pltpu.SemaphoreType.DMA((32,)),
            pltpu.SemaphoreType.DMA((len(steps),)),
        ],
        flops=2 * TILE * D * 3 * OWN,
        limit=60,
    )


def rim_rows(scalars, own_qkv, sources, starts, pieces):
    def kernel(s_ref, q_ref, *refs):
        at = len(sources)
        x_refs = refs[:at]
        w_refs = refs[at : at + 5]
        last_ref, first_ref, w, x, w_sem, x_sem, q_sem = refs[at + 5 :]
        copies = []
        for part in range(2):
            copies += load_weights(s_ref, w_refs, w, part, OWN, 2 * OWN, w_sem, part * 16)
        for r, (source, *rows) in enumerate(starts):
            for n, start in enumerate(rows):
                copies.append(
                    pltpu.make_async_copy(
                        x_refs[source].at[pl.ds(start, LAT)], x.at[r, pl.ds(n * LAT, LAT)], x_sem.at[2 * r + n]
                    )
                )
                copies[-1].start()
        for n, (ref, start) in enumerate(((first_ref, 0), (last_ref, TILE - LAT))):
            copies.append(
                pltpu.make_async_copy(
                    q_ref.at[pl.ds(start, LAT), pl.ds(OWN, 2 * OWN)], ref.at[pl.ds(0, LAT)], q_sem.at[n]
                )
            )
            copies[-1].start()
        for copy in copies:
            copy.wait()
        total = None
        for r in range(4):
            product = jnp.dot(x[r], weight_of(w, s_ref[r], OWN, 2 * OWN), preferred_element_type=F32)
            total = product if total is None else total + product
        out = total.astype(BF16)
        first_ref[LAT:, :] = out[:LAT]
        last_ref[LAT:, :] = out[LAT:]

    args = [own_qkv, *sources, *pieces]
    return call(
        kernel,
        [jax.ShapeDtypeStruct((2 * LAT, 2 * OWN), BF16)] * 2,
        *args,
        scalars=scalars,
        specs=[ANY] * len(args),
        scratch=[
            pltpu.VMEM((1536, 2304), BF16),
            pltpu.VMEM((4, 2 * LAT, BLOCK), BF16),
            pltpu.SemaphoreType.DMA((32,)),
            pltpu.SemaphoreType.DMA((8,)),
            pltpu.SemaphoreType.DMA((2,)),
        ],
        flops=4 * LAT * D * 2 * OWN,
        limit=60,
    )


def attend(scalars, qkv, left, right, parts, *others):
    def kernel(s_ref, q_ref, k_ref, v_ref, lk, lv, rk, rv, *refs):
        out_refs = refs[len(others) : -2]
        keys, values = refs[-2:]
        keys[0:LAT, :] = lk[...]
        keys[LAT : LAT + TILE, :] = k_ref[...]
        keys[LAT + TILE :, :] = rk[...]
        values[0:LAT, 0:HD] = lv[...]
        values[LAT : LAT + TILE, 0:HD] = v_ref[...]
        values[LAT + TILE :, 0:HD] = rv[...]
        values[:, HD:] = jnp.ones((TILE + 2 * LAT, HD), BF16)
        for m in range(4):
            scores = lax.dot_general(
                q_ref[pl.ds(m * 256, 256), :],
                keys[...],
                (((1,), (1,)), ((), ())),
                preferred_element_type=F32,
            )
            top = jnp.max(scores, axis=-1, keepdims=True)
            probs = jnp.exp2((scores - top) * SCALE).astype(BF16)
            mixed = jnp.dot(probs, values[...], preferred_element_type=F32)
            rows = pl.ds(m * 256 % (TILE // parts), 256)
            out_refs[m * parts // 4][rows, :] = (mixed[:, :HD] / mixed[:, HD:]).astype(BF16)

    def column(first):
        return pl.BlockSpec((TILE, HD), lambda h, s: (0, first + h))

    def rim(which, first):
        return pl.BlockSpec((LAT, HD), lambda h, s: (s[which], first + h))

    args = [qkv, qkv, qkv, left, left, right, right, *others]
    return call(
        kernel,
        [jax.ShapeDtypeStruct((TILE // parts, OWN), BF16)] * parts,
        *args,
        scalars=scalars,
        specs=[column(0), column(3), column(6), rim(0, 0), rim(0, 3), rim(1, 0), rim(1, 3)] + [ANY] * len(others),
        out_specs=[pl.BlockSpec((TILE // parts, HD), lambda h, s: (0, h))] * parts,
        scratch=[pltpu.VMEM((TILE + 2 * LAT, HD), BF16), pltpu.VMEM((TILE + 2 * LAT, 2 * HD), BF16)],
        flops=4 * TILE * 1280 * OWN,
        grid=(3,),
    )


def out_project(scalars, start, blocks, weights, dtype):
    counts = [len(block) for block in blocks]
    flat = [part for block in blocks for part in block]

    def kernel(s_ref, *refs):
        t_ref, w_ref, out_ref, a, w, sem, w_sem = refs[len(flat) :]
        copies = []
        for r in range(4):
            j = s_ref[r]
            rows = pl.ds(pl.multiple_of((j % 4) * OWN, 128), OWN)
            lanes = pl.ds(pl.multiple_of((j // 4) * BLOCK, 128), BLOCK)
            copies.append(pltpu.make_async_copy(w_ref.at[rows, lanes], w.at[pl.ds(r * OWN, OWN)], w_sem.at[r]))
            copies[-1].start()
        at = 0
        for r, n in enumerate(counts):
            for i in range(n):
                rows = pl.ds(i * (TILE // n), TILE // n)
                target = a.at[rows, pl.ds(r * OWN, OWN)]
                copies.append(pltpu.make_async_copy(refs[at], target, sem.at[at]))
                copies[-1].start()
                at += 1
        for copy in copies:
            copy.wait()
        for m in range(4):
            rows = pl.ds(m * 256, 256)
            total = jnp.dot(a[rows, :], w[...], preferred_element_type=F32)
            out_ref[rows, :] = (t_ref[rows, :].astype(F32) + total).astype(dtype)

    return call(
        kernel,
        jax.ShapeDtypeStruct((TILE, BLOCK), dtype),
        *flat,
        start,
        weights,
        scalars=scalars,
        specs=[ANY] * len(flat) + [INNER, ANY],
        scratch=[
            pltpu.VMEM((TILE, 4 * OWN), BF16),
            pltpu.VMEM((4 * OWN, BLOCK), BF16),
            pltpu.SemaphoreType.DMA((len(flat),)),
            pltpu.SemaphoreType.DMA((4,)),
        ],
        flops=4 * TILE * OWN * BLOCK,
        limit=24,
    )


def head_partial(scalars, mine, other, gain, weights):
    rows = TILE

    def kernel(s_ref, a_ref, b_ref, g_ref, w_ref, keep_ref, send_ref, shift_ref, own_ref, sent_ref):
        yl, core = s_ref[0], s_ref[1]

        def gain_of(which):
            return g_ref[:, pl.ds(pl.multiple_of(yl * 1536 + which * BLOCK, 128), BLOCK)]

        def weight(which, first):
            return w_ref[pl.ds(pl.multiple_of(which * BLOCK, 128), BLOCK), pl.ds(first, 256)]

        gains = [gain_of(core), gain_of(1 - core)]
        parts = []
        columns = []
        place = lax.broadcasted_iota(jnp.int32, (256, 128), 1)
        for m in range(rows // 256):
            part = pl.ds(m * 256, 256)
            a = a_ref[part, :].astype(F32)
            b = b_ref[part, :].astype(F32)
            mean = (jnp.sum(a, axis=-1, keepdims=True) + jnp.sum(b, axis=-1, keepdims=True)) * (1.0 / 1536)
            a = a - mean
            b = b - mean
            spread = jnp.sum(a * a, axis=-1, keepdims=True) + jnp.sum(b * b, axis=-1, keepdims=True)
            parts.append(((a * gains[0]).astype(BF16), (b * gains[1]).astype(BF16)))
            columns.append(jnp.where(place == 0, mean, jnp.where(place == 1, spread, 0.0)))
        stats = jnp.transpose(jnp.concatenate(columns, axis=0))[0:8]
        own_ref[...] = stats
        shifts = []
        for lanes in (yl * 256, (1 - yl) * 256):
            lanes = pl.multiple_of(lanes, 128)
            mine_weight, other_weight = weight(core, lanes), weight(1 - core, lanes)
            target = send_ref if len(shifts) else keep_ref
            for m, (a, b) in enumerate(parts):
                product = jnp.dot(a, mine_weight, preferred_element_type=F32)
                product += jnp.dot(b, other_weight, preferred_element_type=F32)
                target[pl.ds(m * 256, 256), :] = product.astype(target.dtype)
            shift = jnp.zeros((8, 256), F32)
            for gain, block in zip(gains, (mine_weight, other_weight)):
                high = gain.astype(BF16)
                low = (gain - high.astype(F32)).astype(BF16)
                for half in (high, low):
                    shift += jnp.dot(jnp.broadcast_to(half, (8, BLOCK)), block, preferred_element_type=F32)
            shifts.append(shift)
        shift_ref[...] = shifts[0]
        line = lax.broadcasted_iota(jnp.int32, (8, 256), 0)
        sent_ref[:, 256:] = stats[:, 256:]
        sent_ref[:, :256] = stats[:, :256] + jnp.where(line == 2, shifts[1], 0.0)

    args = [mine, other, gain, weights]
    return call(
        kernel,
        (
            jax.ShapeDtypeStruct((rows, 256), F32),
            jax.ShapeDtypeStruct((rows, 256), BF16),
            jax.ShapeDtypeStruct((8, 256), F32),
            jax.ShapeDtypeStruct((8, rows), F32),
            jax.ShapeDtypeStruct((8, rows), F32),
        ),
        *args,
        scalars=scalars,
        specs=[INNER] * 3 + [pl.BlockSpec((1536, 512), lambda i, s: (0, 3))],
        grid=(1,),
        limit=24,
    )


def combine(kept, received, shift, own, theirs):
    def kernel(s_ref, k_ref, r_ref, shift_ref, o_ref, t_ref, out_ref):
        pad = jnp.zeros((112, TILE), F32)
        both = jnp.transpose(jnp.concatenate([o_ref[...], t_ref[...], pad], axis=0))
        mean_a, spread_a = both[:, 0:1], both[:, 1:2]
        mean_b, spread_b = both[:, 8:9], both[:, 9:10]
        half = (mean_a - mean_b) * 0.5
        spread = (spread_a + spread_b + half * half * D) * (1.0 / D)
        scale = lax.rsqrt(spread + EPS)
        step = shift_ref[...][0:1] - t_ref[...][2:3, :256]
        out_ref[...] = (k_ref[...] + r_ref[...].astype(F32) + half * step) * scale

    return call(
        kernel,
        jax.ShapeDtypeStruct((TILE, 256), F32),
        kept,
        received,
        shift,
        own,
        theirs,
        scalars=jnp.zeros((1,), jnp.int32),
    )


def shards(
    tokens, norm_gain, query_weight, key_weight, value_weight, out_weight, head_gain, head_weight
):
    tile = lax.axis_index("tile")
    var = lax.axis_index("var")
    yh, place = tile // 16, tile % 16
    x, z = place // 4, place % 4
    yl, c = var // 2, var % 2

    halves_of_y = jnp.stack([yh, yl]).astype(jnp.int32)
    mine, leaving = leaving_weights(halves_of_y, query_weight, key_weight, value_weight, out_weight, head_weight)
    got = send(leaving, far)

    raw = tokens.astype(F32)
    mean = jnp.mean(raw, axis=-1)
    spread = jnp.sum((raw - mean[:, None]) ** 2, axis=-1)
    stats = joined([(jnp.stack([mean, spread]), 0, 2)], leaving)
    all_stats = [stats, send(stats, other_core), send(stats, near), send(stats, near_other_core)]
    total_mean = (all_stats[0][0] + all_stats[1][0] + all_stats[2][0] + all_stats[3][0]) * 0.25
    total = sum(s[1] + BLOCK * (s[0] - total_mean) ** 2 for s in all_stats) * (1.0 / D)
    gain = lax.dynamic_slice_in_dim(norm_gain, var * BLOCK, BLOCK)
    normed = ((raw - total_mean[:, None]) * lax.rsqrt(total + EPS)[:, None] * gain).astype(BF16)

    inner = TILE - 2 * LAT
    flip = lambda value: send(value, other_core)
    normed_flip = flip(normed)
    shard, head_keep, head_leaving = paired_weights(halves_of_y, mine, got, head_weight, normed_flip)
    rim = joined([(normed, 0, LAT), (normed, TILE - LAT, LAT)], shard)
    rim_and_heads = joined([(normed, 0, LAT), (normed, TILE - LAT, LAT), (head_leaving, 0, 96)])
    steps = [send(shard, along(True, step)) for step in (1, -1, 2)]
    near_rim = send(rim_and_heads, near)
    diagonal_rim = send(rim, diagonal)

    line = joined([(part, 0, 96) for part in (shard, *steps)], near_rim, diagonal_rim)
    middle = joined([(normed, LAT, inner)], line)
    left = send(line, along(False, 1))
    right = send(line, along(False, -1))
    near_inner = send(middle, near)
    diagonal_inner = send(middle, diagonal)

    stage = [value[:16, :128] for value in (left, right, near_inner, diagonal_inner)]
    far_left = send(joined([(left, 0, 192)], *stage), along(False, 1))
    far_right = send(joined([(right, 192, 192)], *stage), along(False, -1))
    far_top = send(joined([(diagonal_rim, 0, LAT), (diagonal_inner, 0, inner // 2)], *stage), near)
    far_bottom = send(joined([(near_inner, inner // 2, inner // 2), (near_rim, LAT, LAT)], *stage), diagonal)
    held = joined([(near_rim, 0, 256), (diagonal_rim, 0, 256), (near_inner, 0, inner), (diagonal_inner, 0, inner)], *stage)
    pieces = (line, left, right, far_left, far_right)
    held_flip = flip(held)

    groups = [list(range(0, 16)), list(range(16, 32))]
    late_weights = lax.all_gather(
        late_rows(halves_of_y, out_weight, got, head_keep, near_rim, *stage),
        "tile", axis_index_groups=groups, axis=0, tiled=True
    )

    offsets = jnp.array([0, -1, 1, 2], jnp.int32)
    second, primary = jnp.meshgrid(offsets, offsets, indexing="ij")
    place_z = jnp.where(c == 0, z + primary, z + second) % 4
    place_x = jnp.where(c == 0, x + second, x + primary) % 4
    places = (place_x * 4 + place_z).reshape(16)

    def table(*entries):
        return jnp.concatenate([jnp.stack(entries), places]).astype(jnp.int32)

    def vars_of(half):
        return 2 * half + c, 2 * half + 1 - c, 2 * (1 - half) + c, 2 * (1 - half) + 1 - c

    def whole(source):
        return [(source, m * 256, m * 256, 256) for m in range(4)]

    def ringed(rims, start, inner, first):
        return [
            (rims, start, 0, LAT),
            (inner, first, LAT, LAT),
            (inner, first + LAT, 256, 256),
            (inner, first + 384, 512, 256),
            (inner, first + 640, 768, LAT),
            (rims, start + LAT, 896, LAT),
        ]

    own_qkv = project(
        table(*vars_of(yl)),
        [normed, normed_flip, held, held_flip],
        [whole(0), whole(1), ringed(2, 0, 2, 512), ringed(3, 0, 3, 512)],
        pieces,
    )
    far_block = joined([(far_top, 0, 512), (far_bottom, 0, 512)], own_qkv)
    far_flip = flip(far_block)
    rest_table = table(*vars_of(1 - yl))
    last_rims, first_rims = rim_rows(
        rest_table,
        own_qkv,
        [held, held_flip, far_block, far_flip],
        [(0, 256, 384), (1, 256, 384), (2, 0, 896), (3, 0, 896)],
        pieces,
    )
    before = send(last_rims, next_place(1))
    behind = send(first_rims, next_place(-1))
    rest_qkv = project(
        rest_table,
        [held, held_flip, far_block, far_flip, last_rims],
        [ringed(0, 256, 0, 1280), ringed(1, 256, 1, 1280), whole(2), whole(3)],
        pieces,
    )

    swap_left = (place == 0).astype(jnp.int32)
    swap_right = (place == 15).astype(jnp.int32)
    own_rims = jnp.stack([swap_left, swap_right])
    rest_rims = 1 - own_rims
    ids = [
        (2 * half + core) * 2 + high_half
        for half, high_half in ((yl, yh), (yl, 1 - yh), (1 - yl, 1 - yh), (1 - yl, yh))
        for core in (c, 1 - c)
    ]
    out_table = jnp.stack(ids).astype(jnp.int32)
    head_table = jnp.stack([yl, c]).astype(jnp.int32)
    all_gain = head_gain[None]
    rest_attended = attend(rest_rims, rest_qkv, before, behind, 1)[0]
    from_far = send(rest_attended, far)
    from_diagonal = send(rest_attended, diagonal)
    own_attended = attend(own_rims, own_qkv, before, behind, 2, rest_attended)
    from_near = [send(part, near) for part in own_attended]
    blocks = []
    for block in (own_attended, [from_far], [from_diagonal], from_near):
        blocks += [block, [flip(part) for part in block]]
    early = out_project(out_table[:4], tokens, blocks[:4], late_weights, F32)
    resid = out_project(out_table[4:], early, blocks[4:], late_weights, BF16)
    kept, partial, shift, own_stats, partial_stats = head_partial(
        head_table, resid, flip(resid), all_gain, late_weights
    )
    return combine(kept, send(partial, near), shift, own_stats, send(partial_stats, near))


def solution(mesh):
    return jax.shard_map(
        shards,
        mesh=mesh,
        in_specs=(
            P("tile", "var"),
            P(),
            P("tile", "var"),
            P("tile", "var"),
            P("tile", "var"),
            P("tile", "var"),
            P(),
            P("tile", "var"),
        ),
        out_specs=P("tile", "var"),
        check_vma=False,
    )
```

```python
import math

import jax
import jax.numpy as jnp
from jax import lax
from jax.experimental import pallas as pl
from jax.experimental.pallas import tpu as pltpu
from jax.sharding import PartitionSpec as P

D = 3072
HD = 128
LAT = 128
TILE = 1024
BLOCK = 768
OWN = 384
EPS = 1e-05
AXES = ("tile", "var")
SCALE = math.log2(math.e) / math.sqrt(HD)
F32 = jnp.float32
BF16 = jnp.bfloat16


def device(yh, x, z, yl, c):
    return ((yh % 2) * 16 + (x % 4) * 4 + (z % 4)) * 4 + (yl % 2) * 2 + (c % 2)


def pairs(move):
    return [
        (device(yh, x, z, yl, c), device(*move(yh, x, z, yl, c)))
        for yh in range(2)
        for x in range(4)
        for z in range(4)
        for yl in range(2)
        for c in range(2)
    ]


def send(value, move):
    return lax.ppermute(value, AXES, pairs(move))


def other_core(yh, x, z, yl, c):
    return yh, x, z, yl, c + 1


def near(yh, x, z, yl, c):
    return yh, x, z, yl + 1, c


def near_other_core(yh, x, z, yl, c):
    return yh, x, z, yl + 1, c + 1


def far(yh, x, z, yl, c):
    return yh + 1, x, z, yl, c


def diagonal(yh, x, z, yl, c):
    return yh + 1, x, z, yl + 1, c


def along(first, step):
    def move(yh, x, z, yl, c):
        if (c == 0) == first:
            return yh, x, z + step, yl, c
        return yh, x + step, z, yl, c

    return move


def next_place(step):
    def move(yh, x, z, yl, c):
        place = (x * 4 + z + step) % 16
        return yh, place // 4, place % 4, yl, c

    return move


def call(kernel, out_shape, *args, scalars, specs=None, scratch=(), flops=0, grid=(), out_specs=None, limit=16):
    whole = pl.BlockSpec(memory_space=pltpu.VMEM)
    out_specs = out_specs or jax.tree.map(lambda _: whole, out_shape)
    return pl.pallas_call(
        kernel,
        out_shape=out_shape,
        grid_spec=pltpu.PrefetchScalarGridSpec(
            num_scalar_prefetch=1,
            grid=grid,
            in_specs=specs or [whole] * len(args),
            out_specs=out_specs,
            scratch_shapes=scratch,
        ),
        compiler_params=pltpu.CompilerParams(vmem_limit_bytes=limit * 2**20),
        cost_estimate=pl.CostEstimate(flops=flops, bytes_accessed=flops // 512, transcendentals=0),
    )(scalars, *args)


ANY = pl.BlockSpec(memory_space=pl.ANY)
INNER = pl.BlockSpec(memory_space=pltpu.VMEM)
def joined(parts, *others):
    total = sum(n for _, _, n in parts)
    shape = parts[0][0].shape

    def kernel(s_ref, *refs):
        out_ref, sem = refs[-2:]
        copies = []
        at = 0
        for i, (_, start, n) in enumerate(parts):
            copies.append(
                pltpu.make_async_copy(refs[i].at[pl.ds(start, n)], out_ref.at[pl.ds(at, n)], sem.at[i])
            )
            copies[-1].start()
            at += n
        for copy in copies:
            copy.wait()

    args = [part[0] for part in parts] + list(others)
    return call(
        kernel,
        jax.ShapeDtypeStruct((total,) + shape[1:], parts[0][0].dtype),
        *args,
        scalars=jnp.zeros((1,), jnp.int32),
        specs=[ANY] * len(args),
        scratch=[pltpu.SemaphoreType.DMA((len(parts),))],
    )


def leaving_weights(scalars, *weights):
    def kernel(s_ref, q_ref, k_ref, v_ref, o_ref, h_ref, mine_ref, send_ref):
        own = pl.ds(pl.multiple_of(s_ref[0] * OWN, 128), OWN)
        other = pl.ds(pl.multiple_of((1 - s_ref[0]) * OWN, 128), OWN)
        for i, ref in enumerate((q_ref, k_ref, v_ref)):
            mine_ref[:, pl.ds(i * OWN, OWN)] = ref[:, own]
            send_ref[:, pl.ds(i * OWN, OWN)] = ref[:, other]
        send_ref[:, 1152:1920] = o_ref[...]
        send_ref[:, 1920:] = h_ref[...]

    return call(
        kernel,
        (jax.ShapeDtypeStruct((96, 1152), BF16), jax.ShapeDtypeStruct((96, 2176), BF16)),
        *weights,
        scalars=scalars,
    )


def paired_weights(scalars, mine, got, head_weight, *others):
    def kernel(s_ref, m_ref, g_ref, h_ref, *refs):
        shard_ref, keep_ref, send_ref = refs[len(others) :]
        yh, same = s_ref[0], s_ref[0] == s_ref[1]
        shard_ref[:, pl.ds(pl.multiple_of(yh * 1152, 128), 1152)] = m_ref[...]
        shard_ref[:, pl.ds(pl.multiple_of((1 - yh) * 1152, 128), 1152)] = g_ref[:, :1152]
        keep_ref[...] = jnp.where(same, h_ref[...], g_ref[:, 1920:])
        send_ref[:, :256] = jnp.where(same, g_ref[:, 1920:], h_ref[...])
        send_ref[:, 256:] = jnp.zeros((96, 512), BF16)

    return call(
        kernel,
        (
            jax.ShapeDtypeStruct((96, 2304), BF16),
            jax.ShapeDtypeStruct((96, 256), BF16),
            jax.ShapeDtypeStruct((96, BLOCK), BF16),
        ),
        mine,
        got,
        head_weight,
        *others,
        scalars=scalars,
        specs=[INNER] * 3 + [ANY] * len(others),
    )


def late_rows(scalars, out_weight, got, keep, near_rim, *others):
    def kernel(s_ref, o_ref, g_ref, k_ref, n_ref, *refs):
        yh, yl = s_ref[0], s_ref[1]
        out_ref = refs[-1]
        out_ref[:, pl.ds(pl.multiple_of(yh * BLOCK, 128), BLOCK)] = o_ref[...]
        out_ref[:, pl.ds(pl.multiple_of((1 - yh) * BLOCK, 128), BLOCK)] = g_ref[:, 1152:1920]
        out_ref[:, pl.ds(pl.multiple_of(1536 + yl * 256, 128), 256)] = k_ref[...]
        out_ref[:, pl.ds(pl.multiple_of(1792 - yl * 256, 128), 256)] = n_ref[256:, :256]

    return call(
        kernel,
        jax.ShapeDtypeStruct((96, 2048), BF16),
        out_weight,
        got,
        keep,
        near_rim,
        *others,
        scalars=scalars,
        specs=[INNER] * 4 + [ANY] * len(others),
    )


PIECES = [range(0, 4), range(4, 8), range(8, 12), range(12, 14), range(14, 16)]


def load_weights(s_ref, refs, target, part, first, width, sem, base):
    lanes = pl.ds(pl.multiple_of(part * 1152 + first, 128), width)
    copies = []
    for ref, numbers in zip(refs, PIECES):
        for n, piece in enumerate(numbers):
            place = pl.ds(pl.multiple_of(s_ref[4 + piece] * 96, 96), 96)
            copies.append(
                pltpu.make_async_copy(ref.at[pl.ds(n * 96, 96), lanes], target.at[place, lanes], sem.at[base + piece])
            )
            copies[-1].start()
    return copies


def weight_of(w, v, first, width):
    lanes = pl.ds(pl.multiple_of((v // 2) * 1152 + first, 128), width)
    return w[pl.ds(pl.multiple_of((v % 2) * BLOCK, 128), BLOCK), lanes]


def project(scalars, sources, plan, pieces):
    steps = [(r,) + entry for r in range(4) for entry in plan[r]]

    def kernel(s_ref, *refs):
        at = len(sources)
        x_refs = refs[:at]
        w_refs = refs[at : at + 5]
        out_ref, w, x, sums, w_sem, x_sem = refs[at + 5 :]
        low = s_ref[0] // 2
        w_copies = []
        x_copies = []
        for part in range(2):
            w_copies.append(load_weights(s_ref, w_refs, w, low if part == 0 else 1 - low, 0, 1152, w_sem, part * 16))
            for m in range(4):
                for i, (r, source, start, target, n) in enumerate(steps):
                    if target // 256 == m and r // 2 == part:
                        copy = pltpu.make_async_copy(
                            x_refs[source].at[pl.ds(start, n)], x.at[r, pl.ds(target, n)], x_sem.at[i]
                        )
                        copy.start()
                        x_copies.append((part, m, copy))
        for part in range(2):
            for copy in w_copies[part]:
                copy.wait()
            for m in range(4):
                for at_part, step, copy in x_copies:
                    if at_part == part and step == m:
                        copy.wait()
                rows = pl.ds(m * 256, 256)
                total = None
                for r in (2 * part, 2 * part + 1):
                    product = jnp.dot(x[r, rows, :], weight_of(w, s_ref[r], 0, 1152), preferred_element_type=F32)
                    total = product if total is None else total + product
                if part == 0:
                    sums[rows, :] = total
                else:
                    out_ref[rows, :] = (total + sums[rows, :]).astype(BF16)

    args = [*sources, *pieces]
    return call(
        kernel,
        jax.ShapeDtypeStruct((TILE, 3 * OWN), BF16),
        *args,
        scalars=scalars,
        specs=[ANY] * len(args),
        scratch=[
            pltpu.VMEM((1536, 2304), BF16),
            pltpu.VMEM((4, TILE, BLOCK), BF16),
            pltpu.VMEM((TILE, 3 * OWN), F32),
            pltpu.SemaphoreType.DMA((32,)),
            pltpu.SemaphoreType.DMA((len(steps),)),
        ],
        flops=2 * TILE * D * 3 * OWN,
        limit=60,
    )


def rim_rows(scalars, own_qkv, sources, starts, pieces):
    def kernel(s_ref, q_ref, *refs):
        at = len(sources)
        x_refs = refs[:at]
        w_refs = refs[at : at + 5]
        last_ref, first_ref, w, x, w_sem, x_sem, q_sem = refs[at + 5 :]
        copies = []
        for part in range(2):
            copies += load_weights(s_ref, w_refs, w, part, OWN, 2 * OWN, w_sem, part * 16)
        for r, (source, *rows) in enumerate(starts):
            for n, start in enumerate(rows):
                copies.append(
                    pltpu.make_async_copy(
                        x_refs[source].at[pl.ds(start, LAT)], x.at[r, pl.ds(n * LAT, LAT)], x_sem.at[2 * r + n]
                    )
                )
                copies[-1].start()
        for n, (ref, start) in enumerate(((first_ref, 0), (last_ref, TILE - LAT))):
            copies.append(
                pltpu.make_async_copy(
                    q_ref.at[pl.ds(start, LAT), pl.ds(OWN, 2 * OWN)], ref.at[pl.ds(0, LAT)], q_sem.at[n]
                )
            )
            copies[-1].start()
        for copy in copies:
            copy.wait()
        total = None
        for r in range(4):
            product = jnp.dot(x[r], weight_of(w, s_ref[r], OWN, 2 * OWN), preferred_element_type=F32)
            total = product if total is None else total + product
        out = total.astype(BF16)
        first_ref[LAT:, :] = out[:LAT]
        last_ref[LAT:, :] = out[LAT:]

    args = [own_qkv, *sources, *pieces]
    return call(
        kernel,
        [jax.ShapeDtypeStruct((2 * LAT, 2 * OWN), BF16)] * 2,
        *args,
        scalars=scalars,
        specs=[ANY] * len(args),
        scratch=[
            pltpu.VMEM((1536, 2304), BF16),
            pltpu.VMEM((4, 2 * LAT, BLOCK), BF16),
            pltpu.SemaphoreType.DMA((32,)),
            pltpu.SemaphoreType.DMA((8,)),
            pltpu.SemaphoreType.DMA((2,)),
        ],
        flops=4 * LAT * D * 2 * OWN,
        limit=60,
    )


def attend(scalars, qkv, left, right, parts, *others):
    sizes = [TILE] + [TILE // parts] * (parts if parts > 1 else 0)

    def kernel(s_ref, q_ref, k_ref, v_ref, lk, lv, rk, rv, *refs):
        out_refs = refs[len(others) : -2]
        keys, values = refs[-2:]
        keys[0:LAT, :] = lk[...]
        keys[LAT : LAT + TILE, :] = k_ref[...]
        keys[LAT + TILE :, :] = rk[...]
        values[0:LAT, 0:HD] = lv[...]
        values[LAT : LAT + TILE, 0:HD] = v_ref[...]
        values[LAT + TILE :, 0:HD] = rv[...]
        values[:, HD:] = jnp.ones((TILE + 2 * LAT, HD), BF16)
        for m in range(4):
            scores = lax.dot_general(
                q_ref[pl.ds(m * 256, 256), :],
                keys[...],
                (((1,), (1,)), ((), ())),
                preferred_element_type=F32,
            )
            top = jnp.max(scores, axis=-1, keepdims=True)
            probs = jnp.exp2((scores - top) * SCALE).astype(BF16)
            mixed = jnp.dot(probs, values[...], preferred_element_type=F32)
            rows = pl.ds(m * 256 % (TILE // parts), 256)
            out = (mixed[:, :HD] / mixed[:, HD:]).astype(BF16)
            out_refs[0][pl.ds(m * 256, 256), :] = out
            if parts > 1:
                out_refs[1 + m * parts // 4][rows, :] = out

    def column(first):
        return pl.BlockSpec((TILE, HD), lambda h, s: (0, first + h))

    def rim(which, first):
        return pl.BlockSpec((LAT, HD), lambda h, s: (s[which], first + h))

    args = [qkv, qkv, qkv, left, left, right, right, *others]
    return call(
        kernel,
        [jax.ShapeDtypeStruct((size, OWN), BF16) for size in sizes],
        *args,
        scalars=scalars,
        specs=[column(0), column(3), column(6), rim(0, 0), rim(0, 3), rim(1, 0), rim(1, 3)] + [ANY] * len(others),
        out_specs=[pl.BlockSpec((size, HD), lambda h, s: (0, h)) for size in sizes],
        scratch=[pltpu.VMEM((TILE + 2 * LAT, HD), BF16), pltpu.VMEM((TILE + 2 * LAT, 2 * HD), BF16)],
        flops=4 * TILE * 1280 * OWN,
        grid=(3,),
    )


def out_project(scalars, start, first, rows, blocks, weights, dtype):
    flat = [(r,) + part for r, block in enumerate(blocks) for part in block]

    def kernel(s_ref, *refs):
        t_ref, w_ref, out_ref, a, w, sem, w_sem = refs[len(flat) :]
        copies = []
        for r in range(4):
            j = s_ref[r]
            place = pl.ds(pl.multiple_of((j % 4) * OWN, 128), OWN)
            lanes = pl.ds(pl.multiple_of((j // 4) * BLOCK, 128), BLOCK)
            copies.append(pltpu.make_async_copy(w_ref.at[place, lanes], w.at[pl.ds(r * OWN, OWN)], w_sem.at[r]))
        for i, (r, _, source, target, n) in enumerate(flat):
            target = a.at[pl.ds(target, n), pl.ds(r * OWN, OWN)]
            copies.append(pltpu.make_async_copy(refs[i].at[pl.ds(source, n)], target, sem.at[i]))
        for copy in copies:
            copy.start()
        for copy in copies:
            copy.wait()
        for m in range(rows // 256):
            part = pl.ds(m * 256, 256)
            total = jnp.dot(a[part, :], w[...], preferred_element_type=F32)
            out_ref[part, :] = (t_ref[part, :].astype(F32) + total).astype(dtype)

    return call(
        kernel,
        jax.ShapeDtypeStruct((rows, BLOCK), dtype),
        *[part[1] for part in flat],
        start,
        weights,
        scalars=scalars,
        specs=[ANY] * len(flat) + [pl.BlockSpec((rows, BLOCK), lambda i, s: (first // rows, 0)), ANY],
        out_specs=pl.BlockSpec((rows, BLOCK), lambda i, s: (0, 0)),
        scratch=[
            pltpu.VMEM((rows, 4 * OWN), BF16),
            pltpu.VMEM((4 * OWN, BLOCK), BF16),
            pltpu.SemaphoreType.DMA((len(flat),)),
            pltpu.SemaphoreType.DMA((4,)),
        ],
        flops=4 * rows * OWN * BLOCK,
        grid=(1,),
        limit=24,
    )


def head_partial(scalars, mine, other, gain, weights):
    rows = mine.shape[0]

    def kernel(s_ref, a_ref, b_ref, g_ref, w_ref, keep_ref, send_ref, shift_ref, own_ref, sent_ref):
        yl, core = s_ref[0], s_ref[1]

        def gain_of(which):
            return g_ref[:, pl.ds(pl.multiple_of(yl * 1536 + which * BLOCK, 128), BLOCK)]

        def weight(which, first):
            return w_ref[pl.ds(pl.multiple_of(which * BLOCK, 128), BLOCK), pl.ds(first, 256)]

        gains = [gain_of(core), gain_of(1 - core)]
        parts = []
        columns = []
        place = lax.broadcasted_iota(jnp.int32, (256, 128), 1)
        for m in range(rows // 256):
            part = pl.ds(m * 256, 256)
            a = a_ref[part, :].astype(F32)
            b = b_ref[part, :].astype(F32)
            mean = (jnp.sum(a, axis=-1, keepdims=True) + jnp.sum(b, axis=-1, keepdims=True)) * (1.0 / 1536)
            a = a - mean
            b = b - mean
            spread = jnp.sum(a * a, axis=-1, keepdims=True) + jnp.sum(b * b, axis=-1, keepdims=True)
            parts.append(((a * gains[0]).astype(BF16), (b * gains[1]).astype(BF16)))
            columns.append(jnp.where(place == 0, mean, jnp.where(place == 1, spread, 0.0)))
        stats = jnp.transpose(jnp.concatenate(columns, axis=0))[0:8]
        own_ref[...] = stats
        shifts = []
        for lanes in (yl * 256, (1 - yl) * 256):
            lanes = pl.multiple_of(lanes, 128)
            mine_weight, other_weight = weight(core, lanes), weight(1 - core, lanes)
            target = send_ref if len(shifts) else keep_ref
            for m, (a, b) in enumerate(parts):
                product = jnp.dot(a, mine_weight, preferred_element_type=F32)
                product += jnp.dot(b, other_weight, preferred_element_type=F32)
                target[pl.ds(m * 256, 256), :] = product.astype(target.dtype)
            shift = jnp.zeros((8, 256), F32)
            for gain, block in zip(gains, (mine_weight, other_weight)):
                high = gain.astype(BF16)
                low = (gain - high.astype(F32)).astype(BF16)
                for half in (high, low):
                    shift += jnp.dot(jnp.broadcast_to(half, (8, BLOCK)), block, preferred_element_type=F32)
            shifts.append(shift)
        shift_ref[...] = shifts[0]
        line = lax.broadcasted_iota(jnp.int32, (8, 256), 0)
        sent_ref[:, 256:] = stats[:, 256:]
        sent_ref[:, :256] = stats[:, :256] + jnp.where(line == 2, shifts[1], 0.0)

    args = [mine, other, gain, weights]
    return call(
        kernel,
        (
            jax.ShapeDtypeStruct((rows, 256), F32),
            jax.ShapeDtypeStruct((rows, 256), BF16),
            jax.ShapeDtypeStruct((8, 256), F32),
            jax.ShapeDtypeStruct((8, rows), F32),
            jax.ShapeDtypeStruct((8, rows), F32),
        ),
        *args,
        scalars=scalars,
        specs=[INNER] * 3 + [pl.BlockSpec((1536, 512), lambda i, s: (0, 3))],
        grid=(1,),
        limit=24,
    )


def combine(halves):
    rows = TILE // 2

    def kernel(s_ref, *refs):
        out_ref = refs[10]
        for h in range(2):
            kept, received, shift_ref, own, theirs = refs[h * 5 : h * 5 + 5]
            pad = jnp.zeros((112, rows), F32)
            both = jnp.transpose(jnp.concatenate([own[...], theirs[...], pad], axis=0))
            mean_a, spread_a = both[:, 0:1], both[:, 1:2]
            mean_b, spread_b = both[:, 8:9], both[:, 9:10]
            half = (mean_a - mean_b) * 0.5
            spread = (spread_a + spread_b + half * half * D) * (1.0 / D)
            scale = lax.rsqrt(spread + EPS)
            step = shift_ref[...][0:1] - theirs[...][2:3, :256]
            out_ref[pl.ds(h * rows, rows), :] = (kept[...] + received[...].astype(F32) + half * step) * scale

    return call(
        kernel,
        jax.ShapeDtypeStruct((TILE, 256), F32),
        *halves[0],
        *halves[1],
        scalars=jnp.zeros((1,), jnp.int32),
    )


def shards(
    tokens, norm_gain, query_weight, key_weight, value_weight, out_weight, head_gain, head_weight
):
    tile = lax.axis_index("tile")
    var = lax.axis_index("var")
    yh, place = tile // 16, tile % 16
    x, z = place // 4, place % 4
    yl, c = var // 2, var % 2

    halves_of_y = jnp.stack([yh, yl]).astype(jnp.int32)
    mine, leaving = leaving_weights(halves_of_y, query_weight, key_weight, value_weight, out_weight, head_weight)
    got = send(leaving, far)

    raw = tokens.astype(F32)
    mean = jnp.mean(raw, axis=-1)
    spread = jnp.sum((raw - mean[:, None]) ** 2, axis=-1)
    stats = joined([(jnp.stack([mean, spread]), 0, 2)], leaving)
    all_stats = [stats, send(stats, other_core), send(stats, near), send(stats, near_other_core)]
    total_mean = (all_stats[0][0] + all_stats[1][0] + all_stats[2][0] + all_stats[3][0]) * 0.25
    total = sum(s[1] + BLOCK * (s[0] - total_mean) ** 2 for s in all_stats) * (1.0 / D)
    gain = lax.dynamic_slice_in_dim(norm_gain, var * BLOCK, BLOCK)
    normed = ((raw - total_mean[:, None]) * lax.rsqrt(total + EPS)[:, None] * gain).astype(BF16)

    inner = TILE - 2 * LAT
    flip = lambda value: send(value, other_core)
    normed_flip = flip(normed)
    shard, head_keep, head_leaving = paired_weights(halves_of_y, mine, got, head_weight, normed_flip)
    rim = joined([(normed, 0, LAT), (normed, TILE - LAT, LAT)], shard)
    rim_and_heads = joined([(normed, 0, LAT), (normed, TILE - LAT, LAT), (head_leaving, 0, 96)])
    steps = [send(shard, along(True, step)) for step in (1, -1, 2)]
    near_rim = send(rim_and_heads, near)
    diagonal_rim = send(rim, diagonal)

    middle = joined([(normed, LAT, inner)], near_rim[:16, :128], diagonal_rim[:16, :128])
    line = joined([(part, 0, 96) for part in (shard, *steps)], near_rim, diagonal_rim, middle[:16, :128])
    left = send(line, along(False, 1))
    right = send(line, along(False, -1))
    near_inner = send(middle, near)
    diagonal_inner = send(middle, diagonal)

    stage = [value[:16, :128] for value in (left, right, near_inner, diagonal_inner)]
    cuts = [joined([(left, 0, 192)], *stage), joined([(right, 192, 192)], *stage)]
    far_left = send(cuts[0], along(False, 1))
    far_right = send(cuts[1], along(False, -1))
    stage = [value[:16, :128] for value in cuts]
    held = joined([(near_rim, 0, 256), (diagonal_rim, 0, 256), (near_inner, 0, inner), (diagonal_inner, 0, inner)], *stage)
    stage = [held[:16, :128]]
    far_top = send(joined([(diagonal_rim, 0, LAT), (diagonal_inner, 0, inner // 2)], *stage), near)
    far_bottom = send(joined([(near_inner, inner // 2, inner // 2), (near_rim, LAT, LAT)], *stage), diagonal)
    pieces = (line, left, right, far_left, far_right)
    held_flip = flip(held)

    groups = [list(range(0, 16)), list(range(16, 32))]
    late_weights = lax.all_gather(
        late_rows(halves_of_y, out_weight, got, head_keep, near_rim, *stage),
        "tile", axis_index_groups=groups, axis=0, tiled=True
    )

    offsets = jnp.array([0, -1, 1, 2], jnp.int32)
    second, primary = jnp.meshgrid(offsets, offsets, indexing="ij")
    place_z = jnp.where(c == 0, z + primary, z + second) % 4
    place_x = jnp.where(c == 0, x + second, x + primary) % 4
    places = (place_x * 4 + place_z).reshape(16)

    def table(*entries):
        return jnp.concatenate([jnp.stack(entries), places]).astype(jnp.int32)

    def vars_of(half):
        return 2 * half + c, 2 * half + 1 - c, 2 * (1 - half) + c, 2 * (1 - half) + 1 - c

    def whole(source):
        return [(source, m * 256, m * 256, 256) for m in range(4)]

    def ringed(rims, start, inner, first):
        return [
            (rims, start, 0, LAT),
            (inner, first, LAT, LAT),
            (inner, first + LAT, 256, 256),
            (inner, first + 384, 512, 256),
            (inner, first + 640, 768, LAT),
            (rims, start + LAT, 896, LAT),
        ]

    own_qkv = project(
        table(*vars_of(yl)),
        [normed, normed_flip, held, held_flip],
        [whole(0), whole(1), ringed(2, 0, 2, 512), ringed(3, 0, 3, 512)],
        pieces,
    )
    far_block = joined([(far_top, 0, 512), (far_bottom, 0, 512)], own_qkv)
    far_flip = flip(far_block)
    rest_table = table(*vars_of(1 - yl))
    last_rims, first_rims = rim_rows(
        rest_table,
        own_qkv,
        [held, held_flip, far_block, far_flip],
        [(0, 256, 384), (1, 256, 384), (2, 0, 896), (3, 0, 896)],
        pieces,
    )
    before = send(last_rims, next_place(1))
    behind = send(first_rims, next_place(-1))
    rest_qkv = project(
        rest_table,
        [held, held_flip, far_block, far_flip, last_rims],
        [ringed(0, 256, 0, 1280), ringed(1, 256, 1, 1280), whole(2), whole(3)],
        pieces,
    )

    swap_left = (place == 0).astype(jnp.int32)
    swap_right = (place == 15).astype(jnp.int32)
    own_rims = jnp.stack([swap_left, swap_right])
    rest_rims = 1 - own_rims
    ids = [
        (2 * half + core) * 2 + high_half
        for half, high_half in ((yl, yh), (1 - yl, yh), (yl, 1 - yh), (1 - yl, 1 - yh))
        for core in (c, 1 - c)
    ]
    out_table = jnp.stack(ids).astype(jnp.int32)
    head_table = jnp.stack([yl, c]).astype(jnp.int32)
    all_gain = head_gain[None]
    rest_attended = attend(rest_rims, rest_qkv, before, behind, 1)[0]
    from_far = send(rest_attended, far)
    from_diagonal = send(rest_attended, diagonal)
    own_attended, *own_parts = attend(own_rims, own_qkv, before, behind, 2, rest_attended)
    from_near = [send(part, near) for part in own_parts]
    blocks = []
    for block in ([own_attended], from_near, [from_far], [from_diagonal]):
        blocks += [block, [flip(part) for part in block]]
    rows = TILE // 2
    whole_block = lambda block: [(part, 0, i * (TILE // len(block)), TILE // len(block)) for i, part in enumerate(block)]
    early = out_project(out_table[:4], tokens, 0, TILE, [whole_block(block) for block in blocks[:4]], late_weights, F32)
    resid = []
    for half in range(2):
        late_blocks = [[(block[0], half * rows, 0, rows)] for block in blocks[4:]]
        resid.append(out_project(out_table[4:], early, half * rows, rows, late_blocks, late_weights, BF16))
    halves = []
    for part in resid:
        kept, partial, shift, own_stats, partial_stats = head_partial(
            head_table, part, flip(part), all_gain, late_weights
        )
        halves.append((kept, send(partial, near), shift, own_stats, send(partial_stats, near)))
    return combine(halves)


def solution(mesh):
    return jax.shard_map(
        shards,
        mesh=mesh,
        in_specs=(
            P("tile", "var"),
            P(),
            P("tile", "var"),
            P("tile", "var"),
            P("tile", "var"),
            P("tile", "var"),
            P(),
            P("tile", "var"),
        ),
        out_specs=P("tile", "var"),
        check_vma=False,
    )
```
